256 devices in a mesh: group: 8 (over z), member: 32 (over x, y, core).
Axes of the slice: x: 4, y: 4, z: 8, core: 2. Of those that a mesh axis runs over, the one named last changes fastest.
Arguments:
- source: bfloat16 [262144, 256], P(('group', 'member')), may hold values from -6 to 6
- target: bfloat16 [65536, 256], P(('group', 'member')), may hold values from -6 to 6
- pair_source: int32 [256, 128], P(('group', 'member')), may hold values from 0 to 3, as said below
- pair_target: int32 [256, 128], P(('group', 'member')), may hold values from 0 to 63, as said below
- pair_count: int32 [256], P(('group', 'member')), may hold values from 4 to 128, as said below
Outputs:
- log_source: float32 [262144], P(('group', 'member'))
- log_target: float32 [65536], P(('group', 'member'))
The draws below stay inside these ranges and needn't reach their ends.
Inputs may be any that keep to these rules, and one draw needn't show every extreme that they name: `pair_source`: each entry is the device's own source tile, 0 to 3; slots 0 to 3 name each of them once, and no (source tile, window tile) pair stands twice on one device. `pair_target`: window index of the pair's target tile; on every device slot 0 names the device's own target tile (index equal to its member index). `pair_count`: at least 4; in every group one device has exactly 128.
All inputs are finite; a program needn't handle non-finite values.
Results may differ from the reference program's by a relative error of at most 0.0031.
Values may be sent and summed in bfloat16 or wider, within the bound.
A program may use at most 128 MiB of HBM per device.

```python
import jax
import jax.numpy as jnp
from jax import lax

DL = 256
PATCH_SAMPLE_SIZE = 256
ST_DEV = 4
ITERS = 2
P_DEV = 128
NS = 262144
NT = 65536
N_GROUP = 8
N_MEMBER = 32
DEVICES = 256


def pair_table(key):
    base_key = jax.random.fold_in(key, 17)

    def one_device(device):
        device_key = jax.random.fold_in(base_key, device)
        orders = jax.vmap(lambda subkey: jax.random.permutation(subkey, 2 * N_MEMBER))(jax.random.split(device_key, ST_DEV))
        member = (device % N_MEMBER).astype(jnp.int32)
        first_order = orders[0].astype(jnp.int32)
        position = jnp.argmax(first_order == member).astype(jnp.int32)
        leading = first_order[0]
        first_order = first_order.at[position].set(leading).at[0].set(member)
        orders = orders.astype(jnp.int32).at[0].set(first_order)
        relabel = jax.random.permutation(jax.random.fold_in(device_key, 5), ST_DEV).astype(jnp.int32)
        targets = orders[:, :N_MEMBER].T.reshape(P_DEV)
        sources = jnp.tile(relabel, N_MEMBER)
        return (sources.astype(jnp.int32), targets.astype(jnp.int32))
    return jax.vmap(one_device)(jnp.arange(DEVICES, dtype=jnp.int32))


def draw_pair_source(key, part):
    return pair_table(key)[0]


def draw_pair_target(key, part):
    return pair_table(key)[1]


def draw_pair_count(key, part):
    count_key = jax.random.fold_in(key, 31)
    counts = jax.random.randint(jax.random.fold_in(count_key, 1), (DEVICES,), ST_DEV, P_DEV // 2 + 1).astype(jnp.int32)
    busiest = jax.random.randint(jax.random.fold_in(count_key, 2), (DEVICES // N_MEMBER,), 0, N_MEMBER).astype(jnp.int32)
    is_busiest = (jnp.arange(N_MEMBER, dtype=jnp.int32)[None, :] == busiest[:, None]).reshape(DEVICES)
    return jnp.where(is_busiest, P_DEV, counts).astype(jnp.int32)


def block_scale(key, dims, shards, least, top_value):
    def one(axis_at, shards_of):
        draws = jax.random.uniform(jax.random.fold_in(jax.random.fold_in(key, 6), axis_at), (shards_of,), jnp.float32, least / len(shards), top_value / len(shards))
        return jnp.repeat(jnp.exp(draws), dims[axis_at] // shards_of).reshape((-1,) + (1,) * (len(dims) - axis_at - 1))

    loudness = one(*shards[0])
    for cut in shards[1:]:
        loudness = loudness * one(*cut)
    return loudness


def normal_values(rng, extent, spread, most, shards=(), kind=jnp.bfloat16):
    entries = jax.random.normal(rng, extent, jnp.float32) * spread
    if len(shards) > 0:
        entries = block_scale(rng, extent, shards, -0.22, 0.18) * entries
    return jnp.clip(entries, min=-most, max=most).astype(kind)


def setup_inputs(seed: int = 0) -> dict:
    keys = jax.random.split(jax.random.key(seed), 6)
    source = normal_values(keys[0], (NS, DL), 1.0, 6.0, ((0, 256),))
    target = normal_values(keys[1], (NT, DL), 1.0, 6.0, ((0, 256),))
    pair_source = draw_pair_source(jax.random.fold_in(keys[5], 71), 0)
    pair_target = draw_pair_target(jax.random.fold_in(keys[5], 71), 0)
    pair_count = draw_pair_count(jax.random.fold_in(keys[5], 71), 0)
    return dict(source=source, target=target, pair_source=pair_source, pair_target=pair_target, pair_count=pair_count)


regularizer_strength = 0.05

def normalize(values):
    floats = values.astype(jnp.float32)
    return (floats / jnp.sqrt(lax.optimization_barrier(jnp.sum(floats * floats, axis=1, keepdims=True)) + 1e-06)).astype(jnp.bfloat16)

def reference(source, target, pair_source, pair_target, pair_count):
    unit_source = normalize(source).reshape(DEVICES, ST_DEV, PATCH_SAMPLE_SIZE, DL)
    unit_target = normalize(target).reshape(DEVICES, PATCH_SAMPLE_SIZE, DL)
    device_ids = jnp.arange(DEVICES, dtype=jnp.int32)
    home_group = device_ids // N_MEMBER
    target_tiles = ((home_group[:, None] + pair_target // N_MEMBER) % N_GROUP * N_MEMBER + pair_target % N_MEMBER).astype(jnp.int32)
    valid_mask = (jnp.arange(P_DEV, dtype=jnp.int32)[None, :] < pair_count[:, None]).astype(jnp.float32)
    scale_target = jnp.ones((DEVICES, PATCH_SAMPLE_SIZE), jnp.float32)
    scale_source = jnp.ones((DEVICES, ST_DEV, PATCH_SAMPLE_SIZE), jnp.float32)
    for sweep_number in range(ITERS):

        def per_device(device_items, scale_target=scale_target):
            sources, source_slots, tile_ids, surviving_indicator = device_items
            partners = unit_target[tile_ids].astype(jnp.float32)
            own_rows = sources[source_slots].astype(jnp.float32)
            similarity_logits = jnp.einsum('pid,pjd->pij', own_rows, partners, precision=lax.Precision.HIGHEST)
            boltzmann_factor_patches = jnp.exp(similarity_logits / regularizer_strength) / PATCH_SAMPLE_SIZE * surviving_indicator[:, None, None]
            boltzmann_factor_patches = lax.optimization_barrier(boltzmann_factor_patches.astype(jnp.bfloat16)).astype(jnp.float32)
            row_parts = jnp.einsum('pij,pj->pi', boltzmann_factor_patches, scale_target[tile_ids], precision=lax.Precision.HIGHEST)
            pick_source = (source_slots[:, None] == jnp.arange(ST_DEV, dtype=jnp.int32)[None, :]).astype(jnp.float32)
            row_sums = jnp.einsum('ps,pi->si', pick_source, row_parts, precision=lax.Precision.HIGHEST)
            source_scale = 1.0 / row_sums
            column_parts = jnp.einsum('pij,pi->pj', boltzmann_factor_patches, source_scale[source_slots], precision=lax.Precision.HIGHEST)
            return (source_scale, column_parts)
        scale_source, column_parts = lax.map(per_device, (unit_source, pair_source, target_tiles, valid_mask))
        columns = jax.ops.segment_sum(column_parts.reshape(DEVICES * P_DEV, PATCH_SAMPLE_SIZE), target_tiles.reshape(DEVICES * P_DEV), num_segments=DEVICES)
        scale_target = ST_DEV / columns
    return (jnp.log(scale_source).reshape(NS), jnp.log(scale_target).reshape(NT))
```

```python
import jax
import jax.numpy as jnp
from jax import lax
from jax.experimental import pallas as pl
from jax.experimental.pallas import tpu as pltpu
from jax.sharding import PartitionSpec as P

MESH = pl.DeviceIdType.MESH
F32, BF16 = jnp.float32, jnp.bfloat16
ROWS_BY_ROWS = (((1,), (1,)), ((), ()))
ROWS_BY_COLUMNS = (((1,), (0,)), ((), ()))
SHARPNESS = 20.0 * 1.4426950408889634
TILE = 256
SOURCES = 4
WINDOW = 64
SLOTS = 128
ORDER = ((0, 0), (0, 1), (0, 3), (1, 0), (0, 2), (1, 1), (1, 3), (1, 2))
BLOCK = {ra: i for i, ra in enumerate(ORDER)}


def place(block, kind, b):
    return block * 8 + kind * 4 + b


def unit(values):
    floats = values.astype(F32)
    return (floats * lax.rsqrt(jnp.sum(floats * floats, axis=1, keepdims=True) + 1e-06)).astype(BF16)


def high_low(x):
    high = x.astype(BF16)
    return high, (x - high.astype(F32)).astype(BF16)


def stacked(x):
    high = x.astype(BF16).astype(F32)
    both = [jnp.broadcast_to(high, (8, x.shape[1])), jnp.broadcast_to(x - high, (8, x.shape[1]))]
    return jnp.concatenate(both, axis=0).astype(BF16)


def kernel(
    source, target, slot_source, slot_target, source_id, target_id, count,
    log_source, log_target,
    units, window, kernels, row_part, listed, part, pick_window, u_rows, row_mask,
    column_out, column_in, scale_in, scale_out, tile_id,
    z_send, z_recv, p_send, p_recv, p2_send, p2_recv, q_send, q_recv, q2_send, q2_recv, d_send, d_recv,
    x_send, x_recv,
):
    z = lax.axis_index("group")
    m = lax.axis_index("member")
    x, y, core = lax.div(m, 8), lax.rem(lax.div(m, 2), 4), lax.rem(m, 2)

    def device(kind, a, b):
        c = core if kind == 0 else 1 - core
        dx = jnp.where(c == 0, a, b)
        dy = jnp.where(c == 0, b, a)
        return (lax.rem(x + dx, 4) * 4 + lax.rem(y + dy, 4)) * 2 + c

    z_next, z_last = lax.rem(z + 1, 8), lax.rem(z + 7, 8)
    p_next, p_last = (z, device(0, 1, 0)), (z, device(0, 3, 0))
    q_next, q_last = (z, device(0, 0, 1)), (z, device(0, 0, 3))
    sibling = (z, device(1, 0, 0))

    barrier = pltpu.get_barrier_semaphore()
    neighbours = (p_next, p_last, q_next, q_last, sibling, (z_next, m), (z_last, m))
    for neighbour in neighbours:
        pl.semaphore_signal(barrier, inc=1, device_id=neighbour, device_id_type=MESH)
    window[place(0, 0, 0)] = unit(target[...])
    pl.semaphore_wait(barrier, len(neighbours))

    def copy(src, dst, send, recv, to):
        return pltpu.make_async_remote_copy(
            src_ref=src, dst_ref=dst, send_sem=send, recv_sem=recv, device_id=to, device_id_type=MESH
        )

    half = TILE // 2

    def z_copy():
        return copy(window.at[place(0, 0, 0)], window.at[place(BLOCK[1, 0], 0, 0)], z_send, z_recv, (z_last, m))

    def p_copy(r, way):
        src, dst = place(BLOCK[r, 0], 0, 0), place(BLOCK[r, 3 if way == 0 else 1], 0, 0)
        return copy(window.at[src], window.at[dst], p_send.at[r, way], p_recv.at[r, way], p_next if way == 0 else p_last)

    def p2_copy(r, way):
        src, dst = place(BLOCK[r, 3 if way == 0 else 1], 0, 0), place(BLOCK[r, 2], 0, 0)
        rows = pl.ds(way * half, half)
        return copy(
            window.at[src, rows], window.at[dst, rows], p2_send.at[r, way], p2_recv.at[r, way],
            p_next if way == 0 else p_last,
        )

    def q_copy(i, way):
        src, dst = place(i, 0, 0), place(i, 0, 3 if way == 0 else 1)
        return copy(window.at[src], window.at[dst], q_send.at[i, way], q_recv.at[i, way], q_next if way == 0 else q_last)

    def q2_copy(i, way):
        src, dst = place(i, 0, 3 if way == 0 else 1), place(i, 0, 2)
        rows = pl.ds(way * half, half)
        return copy(
            window.at[src, rows], window.at[dst, rows], q2_send.at[i, way], q2_recv.at[i, way],
            q_next if way == 0 else q_last,
        )

    def d_copy(i, b):
        return copy(
            window.at[place(i, 0, b)], window.at[place(i, 1, b)], d_send.at[i, b], d_recv.at[i, b], sibling
        )

    def spread(i):
        q_copy(i, 0).start()
        q_copy(i, 1).start()
        d_copy(i, 0).start()

    z_copy().start()
    p_copy(0, 0).start()
    p_copy(0, 1).start()
    spread(0)

    @pl.loop(0, SOURCES)
    def _(s):
        rows = pl.ds(pl.multiple_of(s * TILE, TILE), TILE)
        units[rows, :] = unit(source[rows, :])

    def window_place(w):
        r, x_to, y_to, core_to = w >> 5, (w >> 3) & 3, (w >> 1) & 3, w & 1
        dx, dy = (x_to - x + 4) & 3, (y_to - y + 4) & 3
        a = jnp.where(core_to == 0, dx, dy)
        b = jnp.where(core_to == 0, dy, dx)
        kind = jnp.where(core_to == core, 0, 1)
        block = jnp.zeros_like(a)
        for (r_, a_), i in BLOCK.items():
            block = jnp.where((r == r_) & (a == a_), i, block)
        return block * 8 + kind * 4 + b

    @pl.loop(0, SLOTS)
    def _(k):
        tile_id[k] = window_place(target_id[0, k]) * SOURCES + source_id[0, k]

    slot = lax.broadcasted_iota(jnp.int32, (1, SLOTS), 1)
    keep = (slot < count[0]).astype(F32)
    places = window_place(slot_target[...])
    tile_row = lax.broadcasted_iota(jnp.int32, (WINDOW, SLOTS), 0)
    window_pick = jnp.where(tile_row == places, keep, 0.0)
    pick_window[...] = window_pick.astype(BF16)
    source_row = lax.broadcasted_iota(jnp.int32, (8, SLOTS), 0)
    source_pick = jnp.where(source_row == slot_source[...], 1.0, 0.0)
    both = (window_pick[:, None, :] * source_pick[None, :, :]).reshape(WINDOW * 8, SLOTS).astype(BF16)
    listed[...] = lax.dot_general(
        both, jnp.ones((SLOTS, 128), BF16), ROWS_BY_COLUMNS, preferred_element_type=F32
    ).reshape(WINDOW, 8, 128)
    mask_row = lax.broadcasted_iota(jnp.int32, (16, TILE), 0)
    for j in range(8):
        row_mask[j] = ((mask_row == j) | (mask_row == j + 8)).astype(F32).astype(BF16)
    row_part[...] = jnp.zeros_like(row_part)

    def make(tiles):
        for s in range(SOURCES):
            rows = pl.ds(s * TILE, TILE)
            total = row_part[rows, :]
            for n in tiles:
                logits = lax.dot_general(units[rows, :], window[n], ROWS_BY_ROWS, preferred_element_type=F32)
                rounded = jnp.exp2(logits * SHARPNESS).astype(BF16)
                kernels[n * SOURCES + s] = rounded
                wide = rounded.astype(F32)
                total += (wide[:, :128] + wide[:, 128:]) * listed[n, s : s + 1, :]
            row_part[rows, :] = total

    def p_arrived(r, way):
        p_copy(r, way).wait_recv()
        p2_copy(r, way).start()
        spread(BLOCK[r, 3 if way == 0 else 1])

    def p2_arrived(r):
        p2_copy(r, 0).wait_recv()
        p2_copy(r, 1).wait_recv()
        spread(BLOCK[r, 2])

    p_arrived(0, 1)
    p_arrived(0, 0)
    z_copy().wait_recv()
    p_copy(1, 0).start()
    p_copy(1, 1).start()
    spread(BLOCK[1, 0])

    @pl.loop(0, 10)
    def _(i):
        @pl.when(i == 1)
        def _():
            p2_arrived(0)

        @pl.when(i == 2)
        def _():
            p_arrived(1, 1)
            p_arrived(1, 0)

        @pl.when(i == 4)
        def _():
            p2_arrived(1)

        @pl.when(i < 8)
        def _():
            q_copy(i, 0).wait_recv()
            q2_copy(i, 0).start()
            d_copy(i, 3).start()
            q_copy(i, 1).wait_recv()
            q2_copy(i, 1).start()
            d_copy(i, 1).start()
            make([place(i, 0, 0), place(i, 0, 1), place(i, 0, 3)])

        @pl.when((i > 0) & (i < 9))
        def _():
            j = i - 1
            q2_copy(j, 0).wait_recv()
            q2_copy(j, 1).wait_recv()
            d_copy(j, 2).start()
            d_copy(j, 0).wait_recv()
            d_copy(j, 3).wait_recv()
            d_copy(j, 1).wait_recv()
            make([place(j, 0, 2), place(j, 1, 0), place(j, 1, 1), place(j, 1, 3)])

        @pl.when(i > 1)
        def _():
            j = i - 2
            d_copy(j, 2).wait_recv()
            make([place(j, 1, 2)])

    def set_source_scale(row_sums):
        for s in range(SOURCES):
            u_rows[s] = stacked(1.0 / row_sums[s])

    def column_sweep():
        @pl.loop(0, SLOTS // 8, unroll=2)
        def _(i):
            total = jnp.zeros((16, TILE), F32)
            for j in range(8):
                k = i * 8 + j
                total += lax.dot_general(
                    u_rows[source_id[0, k]] * row_mask[j], kernels[tile_id[k]], ROWS_BY_COLUMNS,
                    preferred_element_type=F32,
                )
            part[pl.ds(pl.multiple_of(i * 8, 8), 8), :] = total[:8] + total[8:]

    def row_sweep():
        @pl.loop(0, SLOTS // 8, unroll=2)
        def _(i):
            total = jnp.zeros((16, TILE), F32)
            for j in range(8):
                k = i * 8 + j
                total += lax.dot_general(
                    stacked(scale_in[tile_id[k] >> 2]) * row_mask[j], kernels[tile_id[k]], ROWS_BY_ROWS,
                    preferred_element_type=F32,
                )
            part[pl.ds(pl.multiple_of(i * 8, 8), 8), :] = total[:8] + total[8:]

    def gathered(picks):
        high, low = high_low(part[...])
        return lax.dot_general(picks, high, ROWS_BY_COLUMNS, preferred_element_type=F32) + lax.dot_general(
            picks, low, ROWS_BY_COLUMNS, preferred_element_type=F32
        )

    def everyone():
        for i, (r, a) in enumerate(ORDER):
            for kind in range(2):
                for b in range(4):
                    n = place(i, kind, b)
                    there = (-a % 4, -b % 4) if kind == 0 else (-b % 4, -a % 4)
                    if n:
                        yield n, r, device(kind, a, b), place(BLOCK[r, there[0]], kind, there[1])

    def all_bytes(ref, sem):
        others = ref.at[pl.ds(1, WINDOW - 1)]
        pltpu.make_async_copy(others, others, sem).wait()

    def column_totals(it):
        columns = gathered(pick_window[...])
        for n in range(WINDOW):
            column_out[it, n] = columns[n : n + 1, :]
        for n, r, member, there in everyone():
            copy(
                column_out.at[it, n], column_in.at[it, there], x_send.at[it], x_recv.at[it],
                (z if r == 0 else z_next, member),
            ).start()
        all_bytes(column_in.at[it], x_recv.at[it])
        return jnp.sum(column_in[it, pl.ds(1, WINDOW - 1)], axis=0) + columns[:1, :]

    high, low = high_low(row_part[...])
    ones = jnp.ones((16, 128), BF16)
    sums = lax.dot_general(ones, high, ROWS_BY_ROWS, preferred_element_type=F32) + lax.dot_general(
        ones, low, ROWS_BY_ROWS, preferred_element_type=F32
    )
    set_source_scale([sums[:1, s * TILE : (s + 1) * TILE] for s in range(SOURCES)])
    column_sweep()
    scale = float(SOURCES) / column_totals(0)
    scale_out[...] = scale
    scale_in[0] = scale
    for n, r, member, there in everyone():
        copy(scale_out, scale_in.at[there], x_send.at[2], x_recv.at[2], (z if r == 0 else z_last, member)).start()
    all_bytes(scale_in, x_recv.at[2])

    row_sweep()
    source_row = lax.broadcasted_iota(jnp.int32, (16, SLOTS), 0)
    picks = jnp.where(source_row == slot_source[...], keep, 0.0).astype(BF16)
    sums = gathered(picks)
    set_source_scale([sums[s : s + 1, :] for s in range(SOURCES)])
    log_source[...] = jnp.log(float(TILE) / sums[:SOURCES, :])
    column_sweep()
    log_target[...] = jnp.log(float(SOURCES) / column_totals(1))

    z_copy().wait_send()
    for way in range(2):
        for r in range(2):
            p_copy(r, way).wait_send()
            p2_copy(r, way).wait_send()

    @pl.loop(0, 8)
    def _(i):
        for way in range(2):
            q_copy(i, way).wait_send()
            q2_copy(i, way).wait_send()
        for b in range(4):
            d_copy(i, b).wait_send()

    all_bytes(column_in.at[0], x_send.at[0])
    all_bytes(column_in.at[1], x_send.at[1])
    all_bytes(scale_in, x_send.at[2])


def shards(source, target, pair_source, pair_target, pair_count):
    vmem, smem = pl.BlockSpec(memory_space=pltpu.VMEM), pl.BlockSpec(memory_space=pltpu.SMEM)
    dma = pltpu.SemaphoreType.DMA
    log_source, log_target = pl.pallas_call(
        kernel,
        out_shape=(
            jax.ShapeDtypeStruct((SOURCES, TILE), F32),
            jax.ShapeDtypeStruct((1, TILE), F32),
        ),
        in_specs=[vmem, vmem, vmem, vmem, smem, smem, smem],
        out_specs=(vmem, vmem),
        scratch_shapes=[
            pltpu.VMEM((SOURCES * TILE, TILE), BF16),
            pltpu.VMEM((WINDOW, TILE, TILE), BF16),
            pltpu.VMEM((WINDOW * SOURCES, TILE, TILE), BF16),
            pltpu.VMEM((SOURCES * TILE, 128), F32),
            pltpu.VMEM((WINDOW, 8, 128), F32),
            pltpu.VMEM((SLOTS, TILE), F32),
            pltpu.VMEM((WINDOW, SLOTS), BF16),
            pltpu.VMEM((SOURCES, 16, TILE), BF16),
            pltpu.VMEM((8, 16, TILE), BF16),
            pltpu.VMEM((2, WINDOW, 1, TILE), F32),
            pltpu.VMEM((2, WINDOW, 1, TILE), F32),
            pltpu.VMEM((WINDOW, 1, TILE), F32),
            pltpu.VMEM((1, TILE), F32),
            pltpu.SMEM((SLOTS,), jnp.int32),
            dma, dma,
            dma((2, 2)), dma((2, 2)),
            dma((2, 2)), dma((2, 2)),
            dma((8, 2)), dma((8, 2)),
            dma((8, 2)), dma((8, 2)),
            dma((8, 4)), dma((8, 4)),
            dma((3,)), dma((3,)),
        ],
        compiler_params=pltpu.CompilerParams(
            collective_id=0, has_side_effects=True, vmem_limit_bytes=60 * 2**20
        ),
    )(source, target, pair_source, pair_target, pair_source, pair_target, pair_count)
    return log_source.reshape(SOURCES * TILE), log_target.reshape(TILE)


def solution(mesh):
    placed = (
        P(("group", "member"), None),
        P(("group", "member"), None),
        P(("group", "member"), None),
        P(("group", "member"), None),
        P(("group", "member")),
    )
    return jax.shard_map(
        shards,
        mesh=mesh,
        in_specs=placed,
        out_specs=(P(("group", "member")), P(("group", "member"))),
        check_vma=False,
    )
```

```python
import jax
import jax.numpy as jnp
from jax import lax
from jax.experimental import pallas as pl
from jax.experimental.pallas import tpu as pltpu
from jax.sharding import PartitionSpec as P

MESH = pl.DeviceIdType.MESH
F32, BF16 = jnp.float32, jnp.bfloat16
ROWS_BY_ROWS = (((1,), (1,)), ((), ()))
ROWS_BY_COLUMNS = (((1,), (0,)), ((), ()))
SHARPNESS = 20.0 * 1.4426950408889634
TILE = 256
SOURCES = 4
WINDOW = 64
SLOTS = 128
ARRIVAL = (
    0, 10, 30, 1000, 100, 3, 1, 20, 110, 130, 1100, 13, 11, 33, 31, 103,
    101, 120, 2, 1010, 1030, 113, 111, 133, 131, 12, 32, 102, 1110, 1130, 23, 21,
    1020, 1003, 1001, 112, 132, 22, 123, 121, 1120, 1013, 1011, 1103, 1101, 1033, 1031, 122,
    1002, 1012, 1032, 1113, 1111, 1133, 1131, 1023, 1021, 1102, 1112, 1132, 1022, 1123, 1121, 1122,
)
PLACE = {(t // 1000, t // 100 % 10, t // 10 % 10, t % 10): n for n, t in enumerate(ARRIVAL)}
GROUP = 8
UNROLL = 16


def place(r, kind, a, b):
    return PLACE[r, kind, a % 4, b % 4]


def unit(values):
    floats = values.astype(F32)
    return (floats * lax.rsqrt(jnp.sum(floats * floats, axis=1, keepdims=True) + 1e-06)).astype(BF16)


def high_low(x):
    high = x.astype(BF16)
    return high, (x - high.astype(F32)).astype(BF16)


def stacked(x):
    high = x.astype(BF16).astype(F32)
    both = [jnp.broadcast_to(high, (8, x.shape[1])), jnp.broadcast_to(x - high, (8, x.shape[1]))]
    return jnp.concatenate(both, axis=0).astype(BF16)


def kernel(
    source, target, slot_source, slot_target, source_id, count,
    row_sums, column_sums,
    units, window, kernels, turned, row_part, listed, part, pick_window, u_rows, row_mask,
    column_out, column_in, scale_in, scale_out, tile_row_id, tile_id, local,
    t_send, t_recv, d_send, d_recv,
    x_send, x_recv,
):
    z = lax.axis_index("group")
    m = lax.axis_index("member")
    x, y, core = lax.div(m, 8), lax.rem(lax.div(m, 2), 4), lax.rem(m, 2)

    def device(kind, a, b):
        c = core if kind == 0 else 1 - core
        dx = jnp.where(c == 0, a, b)
        dy = jnp.where(c == 0, b, a)
        return (lax.rem(x + dx, 4) * 4 + lax.rem(y + dy, 4)) * 2 + c

    z_next, z_last = lax.rem(z + 1, 8), lax.rem(z + 7, 8)
    sibling = (z, device(1, 0, 0))
    devices = {
        "p+": (z, device(0, 1, 0)), "p-": (z, device(0, 3, 0)), "q+": (z, device(0, 0, 1)), "q-": (z, device(0, 0, 3)),
        "z-": (z_last, m),
    }

    barrier = pltpu.get_barrier_semaphore()
    neighbours = (*devices.values(), (z_next, m), sibling)
    for neighbour in neighbours:
        pl.semaphore_signal(barrier, inc=1, device_id=neighbour, device_id_type=MESH)
    window[0] = unit(target[...])
    pl.semaphore_wait(barrier, len(neighbours))

    def copy(src, dst, send, recv, to):
        return pltpu.make_async_remote_copy(
            src_ref=src, dst_ref=dst, send_sem=send, recv_sem=recv, device_id=to, device_id_type=MESH
        )

    half = TILE // 2
    sends = []

    def tile_copy(src, dst, to, rows=None):
        key = (src, dst, to, rows)
        if key not in sends:
            sends.append(key)
        i = sends.index(key)
        at = pl.ds(0, TILE) if rows is None else pl.ds(rows * half, half)
        return copy(window.at[place(*src), at], window.at[place(*dst), at], t_send.at[i], t_recv.at[i], devices[to])

    def p(r, way):
        return tile_copy((r, 0, 0, 0), (r, 0, 3 if way == 0 else 1, 0), "p+" if way == 0 else "p-")

    def p2(way):
        return tile_copy((0, 0, 3 if way == 0 else 1, 0), (0, 0, 2, 0), "p+" if way == 0 else "p-", way)

    def q(r, a, way):
        return tile_copy((r, 0, a, 0), (r, 0, a, 3 if way == 0 else 1), "q+" if way == 0 else "q-")

    def q2(a, way):
        return tile_copy((0, 0, a, 3 if way == 0 else 1), (0, 0, a, 2), "q+" if way == 0 else "q-", way)

    def down(a, b):
        return tile_copy((0, 0, a, b), (1, 0, a, b), "z-")

    def across(r, a, b):
        n = place(r, 0, a, b)
        return copy(window.at[n], window.at[place(r, 1, a, b)], d_send.at[n], d_recv.at[n], sibling)

    def spread(r, a):
        q(r, a, 0).start()
        q(r, a, 1).start()
        across(r, a, 0).start()

    p(0, 0).start()
    p(0, 1).start()
    down(0, 0).start()
    spread(0, 0)

    @pl.loop(0, SOURCES)
    def _(s):
        rows = pl.ds(pl.multiple_of(s * TILE, TILE), TILE)
        units[s] = unit(source[rows, :])

    slots = slot_target[...]
    r, x_to, y_to, core_to = slots >> 5, (slots >> 3) & 3, (slots >> 1) & 3, slots & 1
    dx, dy = (x_to - x + 4) & 3, (y_to - y + 4) & 3
    code = r * 32 + jnp.where(core_to == core, 0, 16) + jnp.where(core_to == 0, dx * 4 + dy, dy * 4 + dx)
    places = jnp.zeros_like(code)
    for (r_, kind, a, b), n in PLACE.items():
        places = jnp.where(code == r_ * 32 + kind * 16 + a * 4 + b, n, places)
    tile_row_id[...] = places * SOURCES + slot_source[...]
    table = pltpu.make_async_copy(tile_row_id, tile_id, local)
    table.start()

    slot = lax.broadcasted_iota(jnp.int32, (1, SLOTS), 1)
    keep = (slot < count[0]).astype(F32)
    tile_row = lax.broadcasted_iota(jnp.int32, (WINDOW, SLOTS), 0)
    window_pick = jnp.where(tile_row == places, keep, 0.0)
    pick_window[...] = window_pick.astype(BF16)
    source_row = lax.broadcasted_iota(jnp.int32, (8, SLOTS), 0)
    source_pick = jnp.where(source_row == slot_source[...], 1.0, 0.0)
    both = (window_pick[:, None, :] * source_pick[None, :, :]).reshape(WINDOW * 8, SLOTS).astype(BF16)
    listed[...] = lax.dot_general(
        both, jnp.ones((SLOTS, 128), BF16), ROWS_BY_COLUMNS, preferred_element_type=F32
    ).reshape(WINDOW, 8, 128)
    mask_row = lax.broadcasted_iota(jnp.int32, (16, TILE), 0)
    for j in range(8):
        row_mask[j] = ((mask_row == j) | (mask_row == j + 8)).astype(F32).astype(BF16)
    row_part[...] = jnp.zeros_like(row_part)

    def make(tiles):
        for s in range(SOURCES):
            rows = pl.ds(s * TILE, TILE)
            total = row_part[rows, :]
            for n in tiles:
                logits = lax.dot_general(units[s], window[n], ROWS_BY_ROWS, preferred_element_type=F32)
                rounded = jnp.exp2(logits * SHARPNESS).astype(BF16)
                kernels[n * SOURCES + s] = rounded
                wide = rounded.astype(F32)
                total += (wide[:, :128] + wide[:, 128:]) * listed[n, s : s + 1, :]
            row_part[rows, :] = total

    arrivals = {}

    def event(*tiles):
        def put(act):
            arrivals[tiles] = act
        return put

    for way in range(2):
        @event((0, 0, 3 if way == 0 else 1, 0))
        def _(way=way):
            p(0, way).wait_recv()
            p2(way).start()
            spread(0, 3 if way == 0 else 1)

        @event((1, 0, 3 if way == 0 else 1, 0))
        def _(way=way):
            p(1, way).wait_recv()
            spread(1, 3 if way == 0 else 1)

        for a in range(4):
            @event((0, 0, a, 3 if way == 0 else 1))
            def _(a=a, way=way):
                q(0, a, way).wait_recv()
                q2(a, way).start()
                across(0, a, 3 if way == 0 else 1).start()

            @event((1, 0, a, 3 if way == 0 else 1))
            def _(a=a, way=way):
                q(1, a, way).wait_recv()
                across(1, a, 3 if way == 0 else 1).start()

    @event((1, 0, 0, 0))
    def _():
        down(0, 0).wait_recv()
        p(1, 0).start()
        p(1, 1).start()
        spread(1, 0)

    @event((0, 0, 2, 0))
    def _():
        p2(0).wait_recv()
        p2(1).wait_recv()
        down(2, 0).start()
        spread(0, 2)

    @event((1, 0, 2, 0))
    def _():
        down(2, 0).wait_recv()
        spread(1, 2)

    for a in range(4):
        @event((0, 0, a, 2))
        def _(a=a):
            q2(a, 0).wait_recv()
            q2(a, 1).wait_recv()
            down(a, 2).start()
            across(0, a, 2).start()

        @event((1, 0, a, 2))
        def _(a=a):
            down(a, 2).wait_recv()
            across(1, a, 2).start()

        for r in range(2):
            for b in range(4):
                @event((r, 1, a, b))
                def _(r=r, a=a, b=b):
                    across(r, a, b).wait_recv()

    acts = {PLACE[tile]: act for (tile,), act in arrivals.items()}

    @pl.loop(0, WINDOW // GROUP)
    def _(i):
        for step in range(WINDOW // GROUP):
            @pl.when(i == step)
            def _(step=step):
                for n in range(step * GROUP, (step + 1) * GROUP):
                    if n:
                        acts[n]()

        make([i * GROUP + t for t in range(GROUP)])

    table.wait()

    def set_source_scale(row_sums):
        for s in range(SOURCES):
            u_rows[s] = stacked(1.0 / row_sums[s])

    def column_sweep():
        @pl.loop(0, SLOTS // 8, unroll=UNROLL)
        def _(i):
            total = jnp.zeros((16, TILE), F32)
            for j in range(8):
                k = i * 8 + j
                total += lax.dot_general(
                    u_rows[source_id[0, k]] * row_mask[j], kernels[tile_id[0, k]], ROWS_BY_COLUMNS,
                    preferred_element_type=F32,
                )
            part[pl.ds(pl.multiple_of(i * 8, 8), 8), :] = total[:8] + total[8:]

    def turn(first):
        @pl.loop(0, SLOTS // 2, unroll=8)
        def _(k):
            k = first + k
            logits = lax.dot_general(
                window[tile_id[0, k] >> 2], units[source_id[0, k]], ROWS_BY_ROWS, preferred_element_type=F32
            )
            turned[k] = jnp.exp2(logits * SHARPNESS).astype(BF16)

    def row_sweep():
        @pl.loop(0, SLOTS // 8, unroll=UNROLL)
        def _(i):
            total = jnp.zeros((16, TILE), F32)
            for j in range(8):
                k = i * 8 + j
                total += lax.dot_general(
                    stacked(scale_in[tile_id[0, k] >> 2]) * row_mask[j], turned[k], ROWS_BY_COLUMNS,
                    preferred_element_type=F32,
                )
            part[pl.ds(pl.multiple_of(i * 8, 8), 8), :] = total[:8] + total[8:]

    def gathered(picks):
        high, low = high_low(part[...])
        return lax.dot_general(picks, high, ROWS_BY_COLUMNS, preferred_element_type=F32) + lax.dot_general(
            picks, low, ROWS_BY_COLUMNS, preferred_element_type=F32
        )

    def everyone():
        for (r, kind, a, b), n in PLACE.items():
            there = (-a, -b) if kind == 0 else (-b, -a)
            if n:
                yield n, r, device(kind, a, b), place(r, kind, *there)

    def all_bytes(ref, sem):
        others = ref.at[pl.ds(1, WINDOW - 1)]
        pltpu.make_async_copy(others, others, sem).wait()

    def column_totals(it):
        columns = gathered(pick_window[...])
        for n in range(WINDOW):
            column_out[it, n] = columns[n : n + 1, :]
        for n, r, member, there in everyone():
            copy(
                column_out.at[it, n], column_in.at[it, there], x_send.at[it], x_recv.at[it],
                (z if r == 0 else z_next, member),
            ).start()
        if it == 0:
            turn(0)
        all_bytes(column_in.at[it], x_recv.at[it])
        return jnp.sum(column_in[it, pl.ds(1, WINDOW - 1)], axis=0) + columns[:1, :]

    high, low = high_low(row_part[...])
    ones = jnp.ones((16, 128), BF16)
    sums = lax.dot_general(ones, high, ROWS_BY_ROWS, preferred_element_type=F32) + lax.dot_general(
        ones, low, ROWS_BY_ROWS, preferred_element_type=F32
    )
    set_source_scale([sums[:1, s * TILE : (s + 1) * TILE] for s in range(SOURCES)])
    column_sweep()
    scale = float(SOURCES) / column_totals(0)
    scale_out[...] = scale
    scale_in[0] = scale
    for n, r, member, there in everyone():
        copy(scale_out, scale_in.at[there], x_send.at[2], x_recv.at[2], (z if r == 0 else z_last, member)).start()
    turn(SLOTS // 2)
    all_bytes(scale_in, x_recv.at[2])

    row_sweep()
    source_row = lax.broadcasted_iota(jnp.int32, (16, SLOTS), 0)
    picks = jnp.where(source_row == slot_source[...], keep, 0.0).astype(BF16)
    sums = gathered(picks)
    set_source_scale([sums[s : s + 1, :] for s in range(SOURCES)])
    for s in range(SOURCES):
        for h in range(2):
            row_sums[pl.ds(2 * s + h, 1), :] = sums[s : s + 1, h * 128 : (h + 1) * 128]
    column_sweep()
    totals = column_totals(1)
    for h in range(2):
        column_sums[pl.ds(h, 1), :] = totals[:, h * 128 : (h + 1) * 128]

    for key in list(sends):
        tile_copy(*key).wait_send()
    for r in range(2):
        for a in range(4):
            for b in range(4):
                across(r, a, b).wait_send()
    all_bytes(column_in.at[0], x_send.at[0])
    all_bytes(column_in.at[1], x_send.at[1])
    all_bytes(scale_in, x_send.at[2])


def shards(source, target, pair_source, pair_target, pair_count):
    vmem, smem = pl.BlockSpec(memory_space=pltpu.VMEM), pl.BlockSpec(memory_space=pltpu.SMEM)
    dma = pltpu.SemaphoreType.DMA
    row_sums, column_sums = pl.pallas_call(
        kernel,
        out_shape=(
            jax.ShapeDtypeStruct((8, 128), F32),
            jax.ShapeDtypeStruct((2, 128), F32),
        ),
        in_specs=[vmem, vmem, vmem, vmem, smem, smem],
        out_specs=(vmem, vmem),
        scratch_shapes=[
            pltpu.VMEM((SOURCES, TILE, TILE), BF16),
            pltpu.VMEM((WINDOW, TILE, TILE), BF16),
            pltpu.VMEM((WINDOW * SOURCES, TILE, TILE), BF16),
            pltpu.VMEM((SLOTS, TILE, TILE), BF16),
            pltpu.VMEM((SOURCES * TILE, 128), F32),
            pltpu.VMEM((WINDOW, 8, 128), F32),
            pltpu.VMEM((SLOTS, TILE), F32),
            pltpu.VMEM((WINDOW, SLOTS), BF16),
            pltpu.VMEM((SOURCES, 16, TILE), BF16),
            pltpu.VMEM((8, 16, TILE), BF16),
            pltpu.VMEM((2, WINDOW, 1, TILE), F32),
            pltpu.VMEM((2, WINDOW, 1, TILE), F32),
            pltpu.VMEM((WINDOW, 1, TILE), F32),
            pltpu.VMEM((1, TILE), F32),
            pltpu.VMEM((1, SLOTS), jnp.int32),
            pltpu.SMEM((1, SLOTS), jnp.int32),
            dma,
            dma((40,)), dma((40,)),
            dma((WINDOW,)), dma((WINDOW,)),
            dma((3,)), dma((3,)),
        ],
        compiler_params=pltpu.CompilerParams(
            collective_id=0, has_side_effects=True, vmem_limit_bytes=62 * 2**20
        ),
    )(source, target, pair_source, pair_target, pair_source, pair_count)
    return jnp.log(float(TILE) / row_sums.reshape(SOURCES * TILE)), jnp.log(float(SOURCES) / column_sums.reshape(TILE))


def solution(mesh):
    placed = (
        P(("group", "member"), None),
        P(("group", "member"), None),
        P(("group", "member"), None),
        P(("group", "member"), None),
        P(("group", "member")),
    )
    return jax.shard_map(
        shards,
        mesh=mesh,
        in_specs=placed,
        out_specs=(P(("group", "member")), P(("group", "member"))),
        check_vma=False,
    )
```

```python
import jax
import jax.numpy as jnp
from jax import lax
from jax.experimental import pallas as pl
from jax.experimental.pallas import tpu as pltpu
from jax.sharding import PartitionSpec as P

MESH = pl.DeviceIdType.MESH
F32, BF16 = jnp.float32, jnp.bfloat16
ROWS_BY_ROWS = (((1,), (1,)), ((), ()))
ROWS_BY_COLUMNS = (((1,), (0,)), ((), ()))
SHARPNESS = 20.0 * 1.4426950408889634
TILE = 256
SOURCES = 4
WINDOW = 64
SLOTS = 128
ARRIVAL = (
    0, 10, 30, 1000, 100, 3, 1, 20, 110, 130, 1100, 13, 11, 33, 31, 103,
    101, 120, 2, 1010, 1030, 113, 111, 133, 131, 12, 32, 102, 1110, 1130, 23, 21,
    1020, 1003, 1001, 112, 132, 22, 123, 121, 1120, 1013, 1011, 1103, 1101, 1033, 1031, 122,
    1002, 1012, 1032, 1113, 1111, 1133, 1131, 1023, 1021, 1102, 1112, 1132, 1022, 1123, 1121, 1122,
)
PLACE = {(t // 1000, t // 100 % 10, t // 10 % 10, t % 10): n for n, t in enumerate(ARRIVAL)}
GROUP = 8
UNROLL = 16


def place(r, kind, a, b):
    return PLACE[r, kind, a % 4, b % 4]


def unit(values):
    floats = values.astype(F32)
    return (floats * lax.rsqrt(jnp.sum(floats * floats, axis=1, keepdims=True) + 1e-06)).astype(BF16)


def high_low(x):
    high = x.astype(BF16)
    return high, (x - high.astype(F32)).astype(BF16)


def stacked(x):
    high = x.astype(BF16).astype(F32)
    both = [jnp.broadcast_to(high, (8, x.shape[1])), jnp.broadcast_to(x - high, (8, x.shape[1]))]
    return jnp.concatenate(both, axis=0).astype(BF16)


def kernel(
    source_in, target_in, pair_source, pair_target, pair_count,
    row_sums, column_sums,
    source, target, slot_source, slot_target, source_id, count, loads,
    units, window, kernels, turned, row_part, listed, part, pick_window, u_rows, row_mask,
    column_out, column_in, scale_in, scale_out, tile_row_id, tile_id, local,
    t_send, t_recv, d_send, d_recv,
    x_send, x_recv,
):
    z = lax.axis_index("group")
    m = lax.axis_index("member")
    x, y, core = lax.div(m, 8), lax.rem(lax.div(m, 2), 4), lax.rem(m, 2)

    def device(kind, a, b):
        c = core if kind == 0 else 1 - core
        dx = jnp.where(c == 0, a, b)
        dy = jnp.where(c == 0, b, a)
        return (lax.rem(x + dx, 4) * 4 + lax.rem(y + dy, 4)) * 2 + c

    z_next, z_last = lax.rem(z + 1, 8), lax.rem(z + 7, 8)
    sibling = (z, device(1, 0, 0))
    devices = {
        "p+": (z, device(0, 1, 0)), "p-": (z, device(0, 3, 0)), "q+": (z, device(0, 0, 1)), "q-": (z, device(0, 0, 3)),
        "z-": (z_last, m),
    }

    barrier = pltpu.get_barrier_semaphore()
    neighbours = (*devices.values(), (z_next, m), sibling)
    for neighbour in neighbours:
        pl.semaphore_signal(barrier, inc=1, device_id=neighbour, device_id_type=MESH)
    inputs = (
        (target_in, target), (source_in, source), (pair_source, source_id), (pair_source, slot_source),
        (pair_target, slot_target), (pair_count, count),
    )
    inputs = [pltpu.make_async_copy(*pair, loads.at[i]) for i, pair in enumerate(inputs)]
    for load in inputs:
        load.start()
    inputs[0].wait()
    window[0] = unit(target[...])
    pl.semaphore_wait(barrier, len(neighbours))

    def copy(src, dst, send, recv, to):
        return pltpu.make_async_remote_copy(
            src_ref=src, dst_ref=dst, send_sem=send, recv_sem=recv, device_id=to, device_id_type=MESH
        )

    half = TILE // 2
    sends = []

    def tile_copy(src, dst, to, rows=None):
        key = (src, dst, to, rows)
        if key not in sends:
            sends.append(key)
        i = sends.index(key)
        at = pl.ds(0, TILE) if rows is None else pl.ds(rows * half, half)
        return copy(window.at[place(*src), at], window.at[place(*dst), at], t_send.at[i], t_recv.at[i], devices[to])

    def p(r, way):
        return tile_copy((r, 0, 0, 0), (r, 0, 3 if way == 0 else 1, 0), "p+" if way == 0 else "p-")

    def p2(way):
        return tile_copy((0, 0, 3 if way == 0 else 1, 0), (0, 0, 2, 0), "p+" if way == 0 else "p-", way)

    def q(r, a, way):
        return tile_copy((r, 0, a, 0), (r, 0, a, 3 if way == 0 else 1), "q+" if way == 0 else "q-")

    def q2(a, way):
        return tile_copy((0, 0, a, 3 if way == 0 else 1), (0, 0, a, 2), "q+" if way == 0 else "q-", way)

    def down(a, b):
        return tile_copy((0, 0, a, b), (1, 0, a, b), "z-")

    def across(r, a, b):
        n = place(r, 0, a, b)
        return copy(window.at[n], window.at[place(r, 1, a, b)], d_send.at[n], d_recv.at[n], sibling)

    def spread(r, a):
        q(r, a, 0).start()
        q(r, a, 1).start()
        across(r, a, 0).start()

    p(0, 0).start()
    p(0, 1).start()
    down(0, 0).start()
    spread(0, 0)

    for load in inputs[1:]:
        load.wait()

    @pl.loop(0, SOURCES)
    def _(s):
        rows = pl.ds(pl.multiple_of(s * TILE, TILE), TILE)
        units[s] = unit(source[rows, :])

    slots = slot_target[...]
    r, x_to, y_to, core_to = slots >> 5, (slots >> 3) & 3, (slots >> 1) & 3, slots & 1
    dx, dy = (x_to - x + 4) & 3, (y_to - y + 4) & 3
    code = r * 32 + jnp.where(core_to == core, 0, 16) + jnp.where(core_to == 0, dx * 4 + dy, dy * 4 + dx)
    places = jnp.zeros_like(code)
    for (r_, kind, a, b), n in PLACE.items():
        places = jnp.where(code == r_ * 32 + kind * 16 + a * 4 + b, n, places)
    tile_row_id[...] = places * SOURCES + slot_source[...]
    table = pltpu.make_async_copy(tile_row_id, tile_id, local)
    table.start()

    slot = lax.broadcasted_iota(jnp.int32, (1, SLOTS), 1)
    keep = (slot < count[0]).astype(F32)
    tile_row = lax.broadcasted_iota(jnp.int32, (WINDOW, SLOTS), 0)
    window_pick = jnp.where(tile_row == places, keep, 0.0)
    pick_window[...] = window_pick.astype(BF16)
    source_row = lax.broadcasted_iota(jnp.int32, (8, SLOTS), 0)
    source_pick = jnp.where(source_row == slot_source[...], 1.0, 0.0)
    both = (window_pick[:, None, :] * source_pick[None, :, :]).reshape(WINDOW * 8, SLOTS).astype(BF16)
    listed[...] = lax.dot_general(
        both, jnp.ones((SLOTS, 128), BF16), ROWS_BY_COLUMNS, preferred_element_type=F32
    ).reshape(WINDOW, 8, 128)
    mask_row = lax.broadcasted_iota(jnp.int32, (16, TILE), 0)
    for j in range(8):
        row_mask[j] = ((mask_row == j) | (mask_row == j + 8)).astype(F32).astype(BF16)
    row_part[...] = jnp.zeros_like(row_part)

    def make(tiles):
        for s in range(SOURCES):
            rows = pl.ds(s * TILE, TILE)
            total = row_part[rows, :]
            for n in tiles:
                logits = lax.dot_general(units[s], window[n], ROWS_BY_ROWS, preferred_element_type=F32)
                rounded = jnp.exp2(logits * SHARPNESS).astype(BF16)
                kernels[n * SOURCES + s] = rounded
                wide = rounded.astype(F32)
                total += (wide[:, :128] + wide[:, 128:]) * listed[n, s : s + 1, :]
            row_part[rows, :] = total

    arrivals = {}

    def event(*tiles):
        def put(act):
            arrivals[tiles] = act
        return put

    for way in range(2):
        @event((0, 0, 3 if way == 0 else 1, 0))
        def _(way=way):
            p(0, way).wait_recv()
            p2(way).start()
            spread(0, 3 if way == 0 else 1)

        @event((1, 0, 3 if way == 0 else 1, 0))
        def _(way=way):
            p(1, way).wait_recv()
            spread(1, 3 if way == 0 else 1)

        for a in range(4):
            @event((0, 0, a, 3 if way == 0 else 1))
            def _(a=a, way=way):
                q(0, a, way).wait_recv()
                q2(a, way).start()
                across(0, a, 3 if way == 0 else 1).start()

            @event((1, 0, a, 3 if way == 0 else 1))
            def _(a=a, way=way):
                q(1, a, way).wait_recv()
                across(1, a, 3 if way == 0 else 1).start()

    @event((1, 0, 0, 0))
    def _():
        down(0, 0).wait_recv()
        p(1, 0).start()
        p(1, 1).start()
        spread(1, 0)

    @event((0, 0, 2, 0))
    def _():
        p2(0).wait_recv()
        p2(1).wait_recv()
        down(2, 0).start()
        spread(0, 2)

    @event((1, 0, 2, 0))
    def _():
        down(2, 0).wait_recv()
        spread(1, 2)

    for a in range(4):
        @event((0, 0, a, 2))
        def _(a=a):
            q2(a, 0).wait_recv()
            q2(a, 1).wait_recv()
            down(a, 2).start()
            across(0, a, 2).start()

        @event((1, 0, a, 2))
        def _(a=a):
            down(a, 2).wait_recv()
            across(1, a, 2).start()

        for r in range(2):
            for b in range(4):
                @event((r, 1, a, b))
                def _(r=r, a=a, b=b):
                    across(r, a, b).wait_recv()

    acts = {PLACE[tile]: act for (tile,), act in arrivals.items()}

    @pl.loop(0, WINDOW // GROUP)
    def _(i):
        for step in range(WINDOW // GROUP):
            @pl.when(i == step)
            def _(step=step):
                for n in range(step * GROUP, (step + 1) * GROUP):
                    if n:
                        acts[n]()

        make([i * GROUP + t for t in range(GROUP)])

    table.wait()

    def set_source_scale(row_sums):
        for s in range(SOURCES):
            u_rows[s] = stacked(1.0 / row_sums[s])

    def column_sweep():
        @pl.loop(0, SLOTS // 8, unroll=UNROLL)
        def _(i):
            total = jnp.zeros((16, TILE), F32)
            for j in range(8):
                k = i * 8 + j
                total += lax.dot_general(
                    u_rows[source_id[0, k]] * row_mask[j], kernels[tile_id[0, k]], ROWS_BY_COLUMNS,
                    preferred_element_type=F32,
                )
            part[pl.ds(pl.multiple_of(i * 8, 8), 8), :] = total[:8] + total[8:]

    def turn(first):
        @pl.loop(0, SLOTS // 2, unroll=8)
        def _(k):
            k = first + k
            logits = lax.dot_general(
                window[tile_id[0, k] >> 2], units[source_id[0, k]], ROWS_BY_ROWS, preferred_element_type=F32
            )
            turned[k] = jnp.exp2(logits * SHARPNESS).astype(BF16)

    def row_sweep():
        @pl.loop(0, SLOTS // 8, unroll=UNROLL)
        def _(i):
            total = jnp.zeros((16, TILE), F32)
            for j in range(8):
                k = i * 8 + j
                total += lax.dot_general(
                    stacked(scale_in[tile_id[0, k] >> 2]) * row_mask[j], turned[k], ROWS_BY_COLUMNS,
                    preferred_element_type=F32,
                )
            part[pl.ds(pl.multiple_of(i * 8, 8), 8), :] = total[:8] + total[8:]

    def gathered(picks):
        high, low = high_low(part[...])
        return lax.dot_general(picks, high, ROWS_BY_COLUMNS, preferred_element_type=F32) + lax.dot_general(
            picks, low, ROWS_BY_COLUMNS, preferred_element_type=F32
        )

    def everyone():
        for (r, kind, a, b), n in PLACE.items():
            there = (-a, -b) if kind == 0 else (-b, -a)
            if n:
                yield n, r, device(kind, a, b), place(r, kind, *there)

    def all_bytes(others, sem):
        pltpu.make_async_copy(others, others, sem).wait()

    other_rows = pl.ds(2, 2 * WINDOW - 2)
    other_tiles = pl.ds(1, WINDOW - 1)

    def sent_tiles():
        for key in list(sends):
            tile_copy(*key).wait_send()
        for r in range(2):
            for a in range(4):
                for b in range(4):
                    across(r, a, b).wait_send()

    def column_totals(it):
        columns = gathered(pick_window[...])
        for h in range(2):
            lanes = columns[:, h * 128 : (h + 1) * 128]
            column_out[it, pl.ds(h, WINDOW, stride=2), :] = lanes
            column_in[it, pl.ds(h, 1), :] = lanes[:1]
        for n, r, member, there in everyone():
            copy(
                column_out.at[it, pl.ds(2 * n, 2)], column_in.at[it, pl.ds(2 * there, 2)], x_send.at[it], x_recv.at[it],
                (z if r == 0 else z_next, member),
            ).start()
        if it == 0:
            turn(0)
            sent_tiles()
        all_bytes(column_in.at[it, other_rows], x_recv.at[it])
        total = jnp.sum(column_in[it].reshape(16, 8, 128), axis=0)
        return total[0:2] + total[2:4] + total[4:6] + total[6:8]

    high, low = high_low(row_part[...])
    ones = jnp.ones((16, 128), BF16)
    sums = lax.dot_general(ones, high, ROWS_BY_ROWS, preferred_element_type=F32) + lax.dot_general(
        ones, low, ROWS_BY_ROWS, preferred_element_type=F32
    )
    set_source_scale([sums[:1, s * TILE : (s + 1) * TILE] for s in range(SOURCES)])
    column_sweep()
    totals = float(SOURCES) / column_totals(0)
    scale = jnp.concatenate([totals[0:1], totals[1:2]], axis=1)
    scale_out[...] = scale
    scale_in[0] = scale
    for n, r, member, there in everyone():
        copy(scale_out, scale_in.at[there], x_send.at[2], x_recv.at[2], (z if r == 0 else z_last, member)).start()
    turn(SLOTS // 2)
    all_bytes(column_in.at[0, other_rows], x_send.at[0])
    all_bytes(scale_in.at[other_tiles], x_recv.at[2])

    row_sweep()
    source_row = lax.broadcasted_iota(jnp.int32, (16, SLOTS), 0)
    picks = jnp.where(source_row == slot_source[...], keep, 0.0).astype(BF16)
    sums = gathered(picks)
    set_source_scale([sums[s : s + 1, :] for s in range(SOURCES)])
    for s in range(SOURCES):
        for h in range(2):
            row_sums[pl.ds(2 * s + h, 1), :] = sums[s : s + 1, h * 128 : (h + 1) * 128]
    column_sweep()
    all_bytes(scale_in.at[other_tiles], x_send.at[2])
    column_sums[...] = column_totals(1)

    all_bytes(column_in.at[1, other_rows], x_send.at[1])


def shards(source, target, pair_source, pair_target, pair_count):
    vmem = pl.BlockSpec(memory_space=pltpu.VMEM)
    dma = pltpu.SemaphoreType.DMA
    row_sums, column_sums = pl.pallas_call(
        kernel,
        out_shape=(
            jax.ShapeDtypeStruct((8, 128), F32),
            jax.ShapeDtypeStruct((2, 128), F32),
        ),
        in_specs=[pl.BlockSpec(memory_space=pl.ANY)] * 5,
        out_specs=(vmem, vmem),
        scratch_shapes=[
            pltpu.VMEM(source.shape, BF16), pltpu.VMEM(target.shape, BF16),
            pltpu.VMEM((1, SLOTS), jnp.int32), pltpu.VMEM((1, SLOTS), jnp.int32),
            pltpu.SMEM((1, SLOTS), jnp.int32), pltpu.SMEM((1,), jnp.int32),
            dma((6,)),
            pltpu.VMEM((SOURCES, TILE, TILE), BF16),
            pltpu.VMEM((WINDOW, TILE, TILE), BF16),
            pltpu.VMEM((WINDOW * SOURCES, TILE, TILE), BF16),
            pltpu.VMEM((SLOTS, TILE, TILE), BF16),
            pltpu.VMEM((SOURCES * TILE, 128), F32),
            pltpu.VMEM((WINDOW, 8, 128), F32),
            pltpu.VMEM((SLOTS, TILE), F32),
            pltpu.VMEM((WINDOW, SLOTS), BF16),
            pltpu.VMEM((SOURCES, 16, TILE), BF16),
            pltpu.VMEM((8, 16, TILE), BF16),
            pltpu.VMEM((2, 2 * WINDOW, 128), F32),
            pltpu.VMEM((2, 2 * WINDOW, 128), F32),
            pltpu.VMEM((WINDOW, 1, TILE), F32),
            pltpu.VMEM((1, TILE), F32),
            pltpu.VMEM((1, SLOTS), jnp.int32),
            pltpu.SMEM((1, SLOTS), jnp.int32),
            dma,
            dma((40,)), dma((40,)),
            dma((WINDOW,)), dma((WINDOW,)),
            dma((3,)), dma((3,)),
        ],
        compiler_params=pltpu.CompilerParams(
            collective_id=0, has_side_effects=True, vmem_limit_bytes=62 * 2**20
        ),
    )(source, target, pair_source, pair_target, pair_count)
    return jnp.log(float(TILE) / row_sums.reshape(SOURCES * TILE)), jnp.log(float(SOURCES) / column_sums.reshape(TILE))


def solution(mesh):
    placed = (
        P(("group", "member"), None),
        P(("group", "member"), None),
        P(("group", "member"), None),
        P(("group", "member"), None),
        P(("group", "member")),
    )
    return jax.shard_map(
        shards,
        mesh=mesh,
        in_specs=placed,
        out_specs=(P(("group", "member")), P(("group", "member"))),
        check_vma=False,
    )
```

```python
import jax
import jax.numpy as jnp
from jax import lax
from jax.experimental import pallas as pl
from jax.experimental.pallas import tpu as pltpu
from jax.sharding import PartitionSpec as P

MESH = pl.DeviceIdType.MESH
F32, BF16 = jnp.float32, jnp.bfloat16
ROWS_BY_ROWS = (((1,), (1,)), ((), ()))
ROWS_BY_COLUMNS = (((1,), (0,)), ((), ()))
SHARPNESS = 20.0 * 1.4426950408889634
TILE = 256
SOURCES = 4
WINDOW = 64
SLOTS = 128
ARRIVAL = (
    0, 10, 30, 1000, 100, 3, 1, 20, 110, 130, 1100, 13, 11, 33, 31, 103,
    101, 120, 2, 1010, 1030, 113, 111, 133, 131, 12, 32, 102, 1110, 1130, 23, 21,
    1020, 1003, 1001, 112, 132, 22, 123, 121, 1120, 1013, 1011, 1103, 1101, 1033, 1031, 122,
    1002, 1012, 1032, 1113, 1111, 1133, 1131, 1023, 1021, 1102, 1112, 1132, 1022, 1123, 1121, 1122,
)
PLACE = {(t // 1000, t // 100 % 10, t // 10 % 10, t % 10): n for n, t in enumerate(ARRIVAL)}
GROUP = 8
UNROLL = 16


def place(r, kind, a, b):
    return PLACE[r, kind, a % 4, b % 4]


def distance(r, kind, a, b):
    return r + 2 * kind + min(a, 4 - a) + min(b, 4 - b)


def unit(values):
    floats = values.astype(F32)
    return (floats * lax.rsqrt(jnp.sum(floats * floats, axis=1, keepdims=True) + 1e-06)).astype(BF16)


def high_low(x):
    high = x.astype(BF16)
    return high, (x - high.astype(F32)).astype(BF16)


def stacked(x):
    high = x.astype(BF16).astype(F32)
    both = [jnp.broadcast_to(high, (8, x.shape[1])), jnp.broadcast_to(x - high, (8, x.shape[1]))]
    return jnp.concatenate(both, axis=0).astype(BF16)


def kernel(
    source_in, target_in, pair_source, pair_target, pair_count,
    row_sums, column_sums,
    source, target, slot_source, slot_target, source_id, count, loads,
    units, window, kernels, turned, row_part, listed, part, pick_window, u_rows, row_mask,
    column_out, column_in, scale_in, scale_out, tile_row_id, tile_id, local,
    t_send, t_recv, d_send, d_recv,
    x_send, x_recv,
):
    z = lax.axis_index("group")
    m = lax.axis_index("member")
    x, y, core = lax.div(m, 8), lax.rem(lax.div(m, 2), 4), lax.rem(m, 2)

    def device(kind, a, b):
        c = core if kind == 0 else 1 - core
        dx = jnp.where(c == 0, a, b)
        dy = jnp.where(c == 0, b, a)
        return (lax.rem(x + dx, 4) * 4 + lax.rem(y + dy, 4)) * 2 + c

    z_next, z_last = lax.rem(z + 1, 8), lax.rem(z + 7, 8)
    sibling = (z, device(1, 0, 0))
    devices = {
        "p+": (z, device(0, 1, 0)), "p-": (z, device(0, 3, 0)), "q+": (z, device(0, 0, 1)), "q-": (z, device(0, 0, 3)),
        "z-": (z_last, m),
    }

    barrier = pltpu.get_barrier_semaphore()
    neighbours = (*devices.values(), (z_next, m), sibling)
    for neighbour in neighbours:
        pl.semaphore_signal(barrier, inc=1, device_id=neighbour, device_id_type=MESH)
    inputs = (
        (target_in, target), (source_in, source), (pair_source, source_id), (pair_source, slot_source),
        (pair_target, slot_target), (pair_count, count),
    )
    inputs = [pltpu.make_async_copy(*pair, loads.at[i]) for i, pair in enumerate(inputs)]
    for load in inputs:
        load.start()
    inputs[0].wait()
    window[0] = unit(target[...])
    pl.semaphore_wait(barrier, len(neighbours))

    def copy(src, dst, send, recv, to):
        return pltpu.make_async_remote_copy(
            src_ref=src, dst_ref=dst, send_sem=send, recv_sem=recv, device_id=to, device_id_type=MESH
        )

    half = TILE // 2
    sends = []

    def tile_copy(src, dst, to, rows=None):
        key = (src, dst, to, rows)
        if key not in sends:
            sends.append(key)
        i = sends.index(key)
        at = pl.ds(0, TILE) if rows is None else pl.ds(rows * half, half)
        return copy(window.at[place(*src), at], window.at[place(*dst), at], t_send.at[i], t_recv.at[i], devices[to])

    def p(r, way):
        return tile_copy((r, 0, 0, 0), (r, 0, 3 if way == 0 else 1, 0), "p+" if way == 0 else "p-")

    def p2(way):
        return tile_copy((0, 0, 3 if way == 0 else 1, 0), (0, 0, 2, 0), "p+" if way == 0 else "p-", way)

    def q(r, a, way):
        return tile_copy((r, 0, a, 0), (r, 0, a, 3 if way == 0 else 1), "q+" if way == 0 else "q-")

    def q2(a, way):
        return tile_copy((0, 0, a, 3 if way == 0 else 1), (0, 0, a, 2), "q+" if way == 0 else "q-", way)

    def down(a, b):
        return tile_copy((0, 0, a, b), (1, 0, a, b), "z-")

    def across(r, a, b):
        n = place(r, 0, a, b)
        return copy(window.at[n], window.at[place(r, 1, a, b)], d_send.at[n], d_recv.at[n], sibling)

    def spread(r, a):
        q(r, a, 0).start()
        q(r, a, 1).start()
        across(r, a, 0).start()

    p(0, 0).start()
    p(0, 1).start()
    down(0, 0).start()
    spread(0, 0)

    for load in inputs[1:]:
        load.wait()

    @pl.loop(0, SOURCES)
    def _(s):
        rows = pl.ds(pl.multiple_of(s * TILE, TILE), TILE)
        units[s] = unit(source[rows, :])

    slots = slot_target[...]
    r, x_to, y_to, core_to = slots >> 5, (slots >> 3) & 3, (slots >> 1) & 3, slots & 1
    dx, dy = (x_to - x + 4) & 3, (y_to - y + 4) & 3
    code = r * 32 + jnp.where(core_to == core, 0, 16) + jnp.where(core_to == 0, dx * 4 + dy, dy * 4 + dx)
    places = jnp.zeros_like(code)
    for (r_, kind, a, b), n in PLACE.items():
        places = jnp.where(code == r_ * 32 + kind * 16 + a * 4 + b, n, places)
    tile_row_id[...] = places * SOURCES + slot_source[...]
    table = pltpu.make_async_copy(tile_row_id, tile_id, local)
    table.start()

    slot = lax.broadcasted_iota(jnp.int32, (1, SLOTS), 1)
    keep = (slot < count[0]).astype(F32)
    tile_row = lax.broadcasted_iota(jnp.int32, (WINDOW, SLOTS), 0)
    window_pick = jnp.where(tile_row == places, keep, 0.0)
    pick_window[...] = window_pick.astype(BF16)
    source_row = lax.broadcasted_iota(jnp.int32, (8, SLOTS), 0)
    source_pick = jnp.where(source_row == slot_source[...], 1.0, 0.0)
    both = (window_pick[:, None, :] * source_pick[None, :, :]).reshape(WINDOW * 8, SLOTS).astype(BF16)
    listed[...] = lax.dot_general(
        both, jnp.ones((SLOTS, 128), BF16), ROWS_BY_COLUMNS, preferred_element_type=F32
    ).reshape(WINDOW, 8, 128)
    mask_row = lax.broadcasted_iota(jnp.int32, (16, TILE), 0)
    for j in range(8):
        row_mask[j] = ((mask_row == j) | (mask_row == j + 8)).astype(F32).astype(BF16)
    row_part[...] = jnp.zeros_like(row_part)

    def make(tiles):
        for s in range(SOURCES):
            rows = pl.ds(s * TILE, TILE)
            total = row_part[rows, :]
            for n in tiles:
                logits = lax.dot_general(units[s], window[n], ROWS_BY_ROWS, preferred_element_type=F32)
                rounded = jnp.exp2(logits * SHARPNESS).astype(BF16)
                kernels[n * SOURCES + s] = rounded
                wide = rounded.astype(F32)
                total += (wide[:, :128] + wide[:, 128:]) * listed[n, s : s + 1, :]
            row_part[rows, :] = total

    arrivals = {}

    def event(*tiles):
        def put(act):
            arrivals[tiles] = act
        return put

    for way in range(2):
        @event((0, 0, 3 if way == 0 else 1, 0))
        def _(way=way):
            p(0, way).wait_recv()
            p2(way).start()
            spread(0, 3 if way == 0 else 1)

        @event((1, 0, 3 if way == 0 else 1, 0))
        def _(way=way):
            p(1, way).wait_recv()
            spread(1, 3 if way == 0 else 1)

        for a in range(4):
            @event((0, 0, a, 3 if way == 0 else 1))
            def _(a=a, way=way):
                q(0, a, way).wait_recv()
                q2(a, way).start()
                across(0, a, 3 if way == 0 else 1).start()

            @event((1, 0, a, 3 if way == 0 else 1))
            def _(a=a, way=way):
                q(1, a, way).wait_recv()
                across(1, a, 3 if way == 0 else 1).start()

    @event((1, 0, 0, 0))
    def _():
        down(0, 0).wait_recv()
        p(1, 0).start()
        p(1, 1).start()
        spread(1, 0)

    @event((0, 0, 2, 0))
    def _():
        p2(0).wait_recv()
        p2(1).wait_recv()
        down(2, 0).start()
        spread(0, 2)

    @event((1, 0, 2, 0))
    def _():
        down(2, 0).wait_recv()
        spread(1, 2)

    for a in range(4):
        @event((0, 0, a, 2))
        def _(a=a):
            q2(a, 0).wait_recv()
            q2(a, 1).wait_recv()
            down(a, 2).start()
            across(0, a, 2).start()

        @event((1, 0, a, 2))
        def _(a=a):
            down(a, 2).wait_recv()
            across(1, a, 2).start()

        for r in range(2):
            for b in range(4):
                @event((r, 1, a, b))
                def _(r=r, a=a, b=b):
                    across(r, a, b).wait_recv()

    acts = {PLACE[tile]: act for (tile,), act in arrivals.items()}

    @pl.loop(0, WINDOW // GROUP)
    def _(i):
        def dispatch(first, last):
            if last - first == 1:
                for n in range(first * GROUP, last * GROUP):
                    if n:
                        acts[n]()
                return
            middle = (first + last) // 2
            pl.when(i < middle)(lambda: dispatch(first, middle))
            pl.when(i >= middle)(lambda: dispatch(middle, last))

        dispatch(0, WINDOW // GROUP)
        make([i * GROUP + t for t in range(GROUP)])

    table.wait()

    def set_source_scale(row_sums):
        for s in range(SOURCES):
            u_rows[s] = stacked(1.0 / row_sums[s])

    def column_sweep():
        @pl.loop(0, SLOTS // 8, unroll=UNROLL)
        def _(i):
            total = jnp.zeros((16, TILE), F32)
            for j in range(8):
                k = i * 8 + j
                total += lax.dot_general(
                    u_rows[source_id[0, k]] * row_mask[j], kernels[tile_id[0, k]], ROWS_BY_COLUMNS,
                    preferred_element_type=F32,
                )
            part[pl.ds(pl.multiple_of(i * 8, 8), 8), :] = total[:8] + total[8:]

    def turn(first):
        @pl.loop(0, SLOTS // 2, unroll=8)
        def _(k):
            k = first + k
            logits = lax.dot_general(
                window[tile_id[0, k] >> 2], units[source_id[0, k]], ROWS_BY_ROWS, preferred_element_type=F32
            )
            turned[k] = jnp.exp2(logits * SHARPNESS).astype(BF16)

    def row_sweep():
        @pl.loop(0, SLOTS // 8, unroll=UNROLL)
        def _(i):
            total = jnp.zeros((16, TILE), F32)
            for j in range(8):
                k = i * 8 + j
                total += lax.dot_general(
                    stacked(scale_in[tile_id[0, k] >> 2]) * row_mask[j], turned[k], ROWS_BY_COLUMNS,
                    preferred_element_type=F32,
                )
            part[pl.ds(pl.multiple_of(i * 8, 8), 8), :] = total[:8] + total[8:]

    def gathered(picks):
        high, low = high_low(part[...])
        return lax.dot_general(picks, high, ROWS_BY_COLUMNS, preferred_element_type=F32) + lax.dot_general(
            picks, low, ROWS_BY_COLUMNS, preferred_element_type=F32
        )

    def everyone():
        for (r, kind, a, b), n in sorted(PLACE.items(), key=lambda item: -distance(*item[0])):
            there = (-a, -b) if kind == 0 else (-b, -a)
            if n:
                yield n, r, device(kind, a, b), place(r, kind, *there)

    def all_bytes(others, sem):
        pltpu.make_async_copy(others, others, sem).wait()

    other_rows = pl.ds(2, 2 * WINDOW - 2)
    other_tiles = pl.ds(1, WINDOW - 1)

    def sent_tiles():
        for key in list(sends):
            tile_copy(*key).wait_send()
        for r in range(2):
            for a in range(4):
                for b in range(4):
                    across(r, a, b).wait_send()

    def column_totals(it):
        columns = gathered(pick_window[...])
        for h in range(2):
            lanes = columns[:, h * 128 : (h + 1) * 128]
            column_out[it, pl.ds(h, WINDOW, stride=2), :] = lanes
            column_in[it, pl.ds(h, 1), :] = lanes[:1]
        for n, r, member, there in everyone():
            copy(
                column_out.at[it, pl.ds(2 * n, 2)], column_in.at[it, pl.ds(2 * there, 2)], x_send.at[it], x_recv.at[it],
                (z if r == 0 else z_next, member),
            ).start()
        if it == 0:
            turn(0)
            sent_tiles()
        all_bytes(column_in.at[it, other_rows], x_recv.at[it])
        total = jnp.sum(column_in[it].reshape(16, 8, 128), axis=0)
        return total[0:2] + total[2:4] + total[4:6] + total[6:8]

    high, low = high_low(row_part[...])
    ones = jnp.ones((16, 128), BF16)
    sums = lax.dot_general(ones, high, ROWS_BY_ROWS, preferred_element_type=F32) + lax.dot_general(
        ones, low, ROWS_BY_ROWS, preferred_element_type=F32
    )
    set_source_scale([sums[:1, s * TILE : (s + 1) * TILE] for s in range(SOURCES)])
    column_sweep()
    totals = float(SOURCES) / column_totals(0)
    scale = jnp.concatenate([totals[0:1], totals[1:2]], axis=1)
    scale_out[...] = scale
    scale_in[0] = scale
    for n, r, member, there in everyone():
        copy(scale_out, scale_in.at[there], x_send.at[2], x_recv.at[2], (z if r == 0 else z_last, member)).start()
    turn(SLOTS // 2)
    all_bytes(column_in.at[0, other_rows], x_send.at[0])
    all_bytes(scale_in.at[other_tiles], x_recv.at[2])

    row_sweep()
    source_row = lax.broadcasted_iota(jnp.int32, (16, SLOTS), 0)
    picks = jnp.where(source_row == slot_source[...], keep, 0.0).astype(BF16)
    sums = gathered(picks)
    set_source_scale([sums[s : s + 1, :] for s in range(SOURCES)])
    for s in range(SOURCES):
        for h in range(2):
            row_sums[pl.ds(2 * s + h, 1), :] = sums[s : s + 1, h * 128 : (h + 1) * 128]
    column_sweep()
    all_bytes(scale_in.at[other_tiles], x_send.at[2])
    column_sums[...] = column_totals(1)

    all_bytes(column_in.at[1, other_rows], x_send.at[1])


def shards(source, target, pair_source, pair_target, pair_count):
    vmem = pl.BlockSpec(memory_space=pltpu.VMEM)
    dma = pltpu.SemaphoreType.DMA
    row_sums, column_sums = pl.pallas_call(
        kernel,
        out_shape=(
            jax.ShapeDtypeStruct((8, 128), F32),
            jax.ShapeDtypeStruct((2, 128), F32),
        ),
        in_specs=[pl.BlockSpec(memory_space=pl.ANY)] * 5,
        out_specs=(vmem, vmem),
        scratch_shapes=[
            pltpu.VMEM(source.shape, BF16), pltpu.VMEM(target.shape, BF16),
            pltpu.VMEM((1, SLOTS), jnp.int32), pltpu.VMEM((1, SLOTS), jnp.int32),
            pltpu.SMEM((1, SLOTS), jnp.int32), pltpu.SMEM((1,), jnp.int32),
            dma((6,)),
            pltpu.VMEM((SOURCES, TILE, TILE), BF16),
            pltpu.VMEM((WINDOW, TILE, TILE), BF16),
            pltpu.VMEM((WINDOW * SOURCES, TILE, TILE), BF16),
            pltpu.VMEM((SLOTS, TILE, TILE), BF16),
            pltpu.VMEM((SOURCES * TILE, 128), F32),
            pltpu.VMEM((WINDOW, 8, 128), F32),
            pltpu.VMEM((SLOTS, TILE), F32),
            pltpu.VMEM((WINDOW, SLOTS), BF16),
            pltpu.VMEM((SOURCES, 16, TILE), BF16),
            pltpu.VMEM((8, 16, TILE), BF16),
            pltpu.VMEM((2, 2 * WINDOW, 128), F32),
            pltpu.VMEM((2, 2 * WINDOW, 128), F32),
            pltpu.VMEM((WINDOW, 1, TILE), F32),
            pltpu.VMEM((1, TILE), F32),
            pltpu.VMEM((1, SLOTS), jnp.int32),
            pltpu.SMEM((1, SLOTS), jnp.int32),
            dma,
            dma((40,)), dma((40,)),
            dma((WINDOW,)), dma((WINDOW,)),
            dma((3,)), dma((3,)),
        ],
        compiler_params=pltpu.CompilerParams(
            collective_id=0, has_side_effects=True, vmem_limit_bytes=62 * 2**20
        ),
    )(source, target, pair_source, pair_target, pair_count)
    return jnp.log(float(TILE) / row_sums.reshape(SOURCES * TILE)), jnp.log(float(SOURCES) / column_sums.reshape(TILE))


def solution(mesh):
    placed = (
        P(("group", "member"), None),
        P(("group", "member"), None),
        P(("group", "member"), None),
        P(("group", "member"), None),
        P(("group", "member")),
    )
    return jax.shard_map(
        shards,
        mesh=mesh,
        in_specs=placed,
        out_specs=(P(("group", "member")), P(("group", "member"))),
        check_vma=False,
    )
```

```python
import jax
import jax.numpy as jnp
from jax import lax
from jax.experimental import pallas as pl
from jax.experimental.pallas import tpu as pltpu
from jax.sharding import PartitionSpec as P

MESH = pl.DeviceIdType.MESH
F32, BF16 = jnp.float32, jnp.bfloat16
ROWS_BY_ROWS = (((1,), (1,)), ((), ()))
ROWS_BY_COLUMNS = (((1,), (0,)), ((), ()))
SHARPNESS = 20.0 * 1.4426950408889634
TILE = 256
SOURCES = 4
WINDOW = 64
SLOTS = 128
ARRIVAL = (
    0, 10, 30, 1000, 100, 3, 1, 20, 110, 130, 1100, 13, 11, 33, 31, 103,
    101, 120, 2, 1010, 1030, 113, 111, 133, 131, 12, 32, 102, 1110, 1130, 23, 21,
    1020, 1003, 1001, 112, 132, 22, 123, 121, 1120, 1013, 1011, 1103, 1101, 1033, 1031, 122,
    1002, 1012, 1032, 1113, 1111, 1133, 1131, 1023, 1021, 1102, 1112, 1132, 1022, 1123, 1121, 1122,
)
PLACE = {(t // 1000, t // 100 % 10, t // 10 % 10, t % 10): n for n, t in enumerate(ARRIVAL)}
GROUP = 8
UNROLL = 16


def place(r, kind, a, b):
    return PLACE[r, kind, a % 4, b % 4]


def distance(r, kind, a, b):
    return r + 2 * kind + min(a, 4 - a) + min(b, 4 - b)


def unit(values):
    floats = values.astype(F32)
    return (floats * lax.rsqrt(jnp.sum(floats * floats, axis=1, keepdims=True) + 1e-06)).astype(BF16)


def high_low(x):
    high = x.astype(BF16)
    return high, (x - high.astype(F32)).astype(BF16)


def stacked(x):
    high = x.astype(BF16).astype(F32)
    both = [jnp.broadcast_to(high, (8, x.shape[1])), jnp.broadcast_to(x - high, (8, x.shape[1]))]
    return jnp.concatenate(both, axis=0).astype(BF16)


def kernel(
    source_in, target_in, pair_source, pair_target, pair_count,
    row_sums, column_sums,
    source, target, slot_source, slot_target, source_id, count, loads,
    units, window, kernels, turned, row_part, listed, part, pick_window, u_rows, row_mask,
    column_out, column_in, scale_in, scale_out, tile_row_id, tile_id, local,
    t_send, t_recv, d_send, d_recv,
    x_send, x_recv,
):
    z = lax.axis_index("group")
    m = lax.axis_index("member")
    x, y, core = lax.div(m, 8), lax.rem(lax.div(m, 2), 4), lax.rem(m, 2)

    def device(kind, a, b):
        c = core if kind == 0 else 1 - core
        dx = jnp.where(c == 0, a, b)
        dy = jnp.where(c == 0, b, a)
        return (lax.rem(x + dx, 4) * 4 + lax.rem(y + dy, 4)) * 2 + c

    z_next, z_last = lax.rem(z + 1, 8), lax.rem(z + 7, 8)
    sibling = (z, device(1, 0, 0))
    devices = {
        "p+": (z, device(0, 1, 0)), "p-": (z, device(0, 3, 0)), "q+": (z, device(0, 0, 1)), "q-": (z, device(0, 0, 3)),
        "z-": (z_last, m),
    }

    barrier = pltpu.get_barrier_semaphore()
    neighbours = (*devices.values(), (z_next, m), sibling)
    for neighbour in neighbours:
        pl.semaphore_signal(barrier, inc=1, device_id=neighbour, device_id_type=MESH)
    inputs = (
        (target_in, target), (source_in, source), (pair_source, source_id), (pair_source, slot_source),
        (pair_target, slot_target), (pair_count, count),
    )
    inputs = [pltpu.make_async_copy(*pair, loads.at[i]) for i, pair in enumerate(inputs)]
    for load in inputs:
        load.start()
    inputs[0].wait()
    window[0] = unit(target[...])
    pl.semaphore_wait(barrier, len(neighbours))

    def copy(src, dst, send, recv, to):
        return pltpu.make_async_remote_copy(
            src_ref=src, dst_ref=dst, send_sem=send, recv_sem=recv, device_id=to, device_id_type=MESH
        )

    half = TILE // 2
    sends = []

    def tile_copy(src, dst, to, rows=None):
        key = (src, dst, to, rows)
        if key not in sends:
            sends.append(key)
        i = sends.index(key)
        at = pl.ds(0, TILE) if rows is None else pl.ds(rows * half, half)
        return copy(window.at[place(*src), at], window.at[place(*dst), at], t_send.at[i], t_recv.at[i], devices[to])

    def p(r, way):
        return tile_copy((r, 0, 0, 0), (r, 0, 3 if way == 0 else 1, 0), "p+" if way == 0 else "p-")

    def p2(way):
        return tile_copy((0, 0, 3 if way == 0 else 1, 0), (0, 0, 2, 0), "p+" if way == 0 else "p-", way)

    def q(r, a, way):
        return tile_copy((r, 0, a, 0), (r, 0, a, 3 if way == 0 else 1), "q+" if way == 0 else "q-")

    def q2(a, way):
        return tile_copy((0, 0, a, 3 if way == 0 else 1), (0, 0, a, 2), "q+" if way == 0 else "q-", way)

    def down(a, b):
        return tile_copy((0, 0, a, b), (1, 0, a, b), "z-")

    def across(r, a, b):
        n = place(r, 0, a, b)
        return copy(window.at[n], window.at[place(r, 1, a, b)], d_send.at[n], d_recv.at[n], sibling)

    def spread(r, a):
        q(r, a, 0).start()
        q(r, a, 1).start()
        across(r, a, 0).start()

    p(0, 0).start()
    p(0, 1).start()
    down(0, 0).start()
    spread(0, 0)

    for load in inputs[1:]:
        load.wait()

    @pl.loop(0, SOURCES)
    def _(s):
        rows = pl.ds(pl.multiple_of(s * TILE, TILE), TILE)
        units[s] = unit(source[rows, :])

    row_part[...] = jnp.zeros_like(row_part)

    def make(tiles):
        for s in range(SOURCES):
            rows = pl.ds(s * TILE, TILE)
            total = row_part[rows, :]
            for n in tiles:
                logits = lax.dot_general(units[s], window[n], ROWS_BY_ROWS, preferred_element_type=F32)
                rounded = jnp.exp2(logits * SHARPNESS).astype(BF16)
                kernels[n * SOURCES + s] = rounded
                wide = rounded.astype(F32)
                total += (wide[:, :128] + wide[:, 128:]) * listed[n, s : s + 1, :]
            row_part[rows, :] = total

    arrivals = {}

    def event(*tiles):
        def put(act):
            arrivals[tiles] = act
        return put

    for way in range(2):
        @event((0, 0, 3 if way == 0 else 1, 0))
        def _(way=way):
            p(0, way).wait_recv()
            p2(way).start()
            spread(0, 3 if way == 0 else 1)

        @event((1, 0, 3 if way == 0 else 1, 0))
        def _(way=way):
            p(1, way).wait_recv()
            spread(1, 3 if way == 0 else 1)

        for a in range(4):
            @event((0, 0, a, 3 if way == 0 else 1))
            def _(a=a, way=way):
                q(0, a, way).wait_recv()
                q2(a, way).start()
                across(0, a, 3 if way == 0 else 1).start()

            @event((1, 0, a, 3 if way == 0 else 1))
            def _(a=a, way=way):
                q(1, a, way).wait_recv()
                across(1, a, 3 if way == 0 else 1).start()

    @event((1, 0, 0, 0))
    def _():
        down(0, 0).wait_recv()
        p(1, 0).start()
        p(1, 1).start()
        spread(1, 0)

    @event((0, 0, 2, 0))
    def _():
        p2(0).wait_recv()
        p2(1).wait_recv()
        down(2, 0).start()
        spread(0, 2)

    @event((1, 0, 2, 0))
    def _():
        down(2, 0).wait_recv()
        spread(1, 2)

    for a in range(4):
        @event((0, 0, a, 2))
        def _(a=a):
            q2(a, 0).wait_recv()
            q2(a, 1).wait_recv()
            down(a, 2).start()
            across(0, a, 2).start()

        @event((1, 0, a, 2))
        def _(a=a):
            down(a, 2).wait_recv()
            across(1, a, 2).start()

        for r in range(2):
            for b in range(4):
                @event((r, 1, a, b))
                def _(r=r, a=a, b=b):
                    across(r, a, b).wait_recv()

    acts = {PLACE[tile]: act for (tile,), act in arrivals.items()}

    early = 3
    for n in range(1, early + 1):
        acts[n]()

    slots = slot_target[...]
    r, x_to, y_to, core_to = slots >> 5, (slots >> 3) & 3, (slots >> 1) & 3, slots & 1
    dx, dy = (x_to - x + 4) & 3, (y_to - y + 4) & 3
    code = r * 32 + jnp.where(core_to == core, 0, 16) + jnp.where(core_to == 0, dx * 4 + dy, dy * 4 + dx)
    places = jnp.zeros_like(code)
    for (r_, kind, a, b), n in PLACE.items():
        places = jnp.where(code == r_ * 32 + kind * 16 + a * 4 + b, n, places)
    tile_row_id[...] = places * SOURCES + slot_source[...]
    table = pltpu.make_async_copy(tile_row_id, tile_id, local)
    table.start()

    slot = lax.broadcasted_iota(jnp.int32, (1, SLOTS), 1)
    keep = (slot < count[0]).astype(F32)
    tile_row = lax.broadcasted_iota(jnp.int32, (WINDOW, SLOTS), 0)
    window_pick = jnp.where(tile_row == places, keep, 0.0)
    pick_window[...] = window_pick.astype(BF16)
    source_row = lax.broadcasted_iota(jnp.int32, (8, SLOTS), 0)
    source_pick = jnp.where(source_row == slot_source[...], 1.0, 0.0)
    both = (window_pick[:, None, :] * source_pick[None, :, :]).reshape(WINDOW * 8, SLOTS).astype(BF16)
    listed[...] = lax.dot_general(
        both, jnp.ones((SLOTS, 128), BF16), ROWS_BY_COLUMNS, preferred_element_type=F32
    ).reshape(WINDOW, 8, 128)
    mask_row = lax.broadcasted_iota(jnp.int32, (16, TILE), 0)
    for j in range(8):
        row_mask[j] = ((mask_row == j) | (mask_row == j + 8)).astype(F32).astype(BF16)
    @pl.loop(0, WINDOW // GROUP)
    def _(i):
        def dispatch(first, last):
            if last - first == 1:
                for n in range(first * GROUP, last * GROUP):
                    if n > early:
                        acts[n]()
                return
            middle = (first + last) // 2
            pl.when(i < middle)(lambda: dispatch(first, middle))
            pl.when(i >= middle)(lambda: dispatch(middle, last))

        dispatch(0, WINDOW // GROUP)
        make([i * GROUP + t for t in range(GROUP)])

    table.wait()

    def set_source_scale(row_sums):
        for s in range(SOURCES):
            u_rows[s] = stacked(1.0 / row_sums[s])

    def column_sweep():
        @pl.loop(0, SLOTS // 8, unroll=UNROLL)
        def _(i):
            total = jnp.zeros((16, TILE), F32)
            for j in range(8):
                k = i * 8 + j
                total += lax.dot_general(
                    u_rows[source_id[0, k]] * row_mask[j], kernels[tile_id[0, k]], ROWS_BY_COLUMNS,
                    preferred_element_type=F32,
                )
            part[pl.ds(pl.multiple_of(i * 8, 8), 8), :] = total[:8] + total[8:]

    def turn(first):
        @pl.loop(0, SLOTS // 2, unroll=8)
        def _(k):
            k = first + k
            logits = lax.dot_general(
                window[tile_id[0, k] >> 2], units[source_id[0, k]], ROWS_BY_ROWS, preferred_element_type=F32
            )
            turned[k] = jnp.exp2(logits * SHARPNESS).astype(BF16)

    def row_sweep():
        @pl.loop(0, SLOTS // 8, unroll=UNROLL)
        def _(i):
            total = jnp.zeros((16, TILE), F32)
            for j in range(8):
                k = i * 8 + j
                total += lax.dot_general(
                    stacked(scale_in[tile_id[0, k] >> 2]) * row_mask[j], turned[k], ROWS_BY_COLUMNS,
                    preferred_element_type=F32,
                )
            part[pl.ds(pl.multiple_of(i * 8, 8), 8), :] = total[:8] + total[8:]

    def gathered(picks):
        high, low = high_low(part[...])
        return lax.dot_general(picks, high, ROWS_BY_COLUMNS, preferred_element_type=F32) + lax.dot_general(
            picks, low, ROWS_BY_COLUMNS, preferred_element_type=F32
        )

    def everyone():
        for (r, kind, a, b), n in sorted(PLACE.items(), key=lambda item: -distance(*item[0])):
            there = (-a, -b) if kind == 0 else (-b, -a)
            if n:
                yield n, r, device(kind, a, b), place(r, kind, *there)

    def all_bytes(others, sem):
        pltpu.make_async_copy(others, others, sem).wait()

    other_rows = pl.ds(2, 2 * WINDOW - 2)
    other_tiles = pl.ds(1, WINDOW - 1)

    def sent_tiles():
        for key in list(sends):
            tile_copy(*key).wait_send()
        for r in range(2):
            for a in range(4):
                for b in range(4):
                    across(r, a, b).wait_send()

    def column_totals(it):
        columns = gathered(pick_window[...])
        for h in range(2):
            lanes = columns[:, h * 128 : (h + 1) * 128]
            column_out[it, pl.ds(h, WINDOW, stride=2), :] = lanes
            column_in[it, pl.ds(h, 1), :] = lanes[:1]
        for n, r, member, there in everyone():
            copy(
                column_out.at[it, pl.ds(2 * n, 2)], column_in.at[it, pl.ds(2 * there, 2)], x_send.at[it], x_recv.at[it],
                (z if r == 0 else z_next, member),
            ).start()
        if it == 0:
            turn(0)
            sent_tiles()
        all_bytes(column_in.at[it, other_rows], x_recv.at[it])
        total = jnp.sum(column_in[it].reshape(16, 8, 128), axis=0)
        return total[0:2] + total[2:4] + total[4:6] + total[6:8]

    high, low = high_low(row_part[...])
    ones = jnp.ones((16, 128), BF16)
    sums = lax.dot_general(ones, high, ROWS_BY_ROWS, preferred_element_type=F32) + lax.dot_general(
        ones, low, ROWS_BY_ROWS, preferred_element_type=F32
    )
    set_source_scale([sums[:1, s * TILE : (s + 1) * TILE] for s in range(SOURCES)])
    column_sweep()
    totals = float(SOURCES) / column_totals(0)
    scale = jnp.concatenate([totals[0:1], totals[1:2]], axis=1)
    scale_out[...] = scale
    scale_in[0] = scale
    for n, r, member, there in everyone():
        copy(scale_out, scale_in.at[there], x_send.at[2], x_recv.at[2], (z if r == 0 else z_last, member)).start()
    turn(SLOTS // 2)
    all_bytes(column_in.at[0, other_rows], x_send.at[0])
    all_bytes(scale_in.at[other_tiles], x_recv.at[2])

    row_sweep()
    source_row = lax.broadcasted_iota(jnp.int32, (16, SLOTS), 0)
    picks = jnp.where(source_row == slot_source[...], keep, 0.0).astype(BF16)
    sums = gathered(picks)
    set_source_scale([sums[s : s + 1, :] for s in range(SOURCES)])
    for s in range(SOURCES):
        for h in range(2):
            row_sums[pl.ds(2 * s + h, 1), :] = sums[s : s + 1, h * 128 : (h + 1) * 128]
    column_sweep()
    all_bytes(scale_in.at[other_tiles], x_send.at[2])
    column_sums[...] = column_totals(1)

    all_bytes(column_in.at[1, other_rows], x_send.at[1])


def shards(source, target, pair_source, pair_target, pair_count):
    vmem = pl.BlockSpec(memory_space=pltpu.VMEM)
    dma = pltpu.SemaphoreType.DMA
    row_sums, column_sums = pl.pallas_call(
        kernel,
        out_shape=(
            jax.ShapeDtypeStruct((8, 128), F32),
            jax.ShapeDtypeStruct((2, 128), F32),
        ),
        in_specs=[pl.BlockSpec(memory_space=pl.ANY)] * 5,
        out_specs=(vmem, vmem),
        scratch_shapes=[
            pltpu.VMEM(source.shape, BF16), pltpu.VMEM(target.shape, BF16),
            pltpu.VMEM((1, SLOTS), jnp.int32), pltpu.VMEM((1, SLOTS), jnp.int32),
            pltpu.SMEM((1, SLOTS), jnp.int32), pltpu.SMEM((1,), jnp.int32),
            dma((6,)),
            pltpu.VMEM((SOURCES, TILE, TILE), BF16),
            pltpu.VMEM((WINDOW, TILE, TILE), BF16),
            pltpu.VMEM((WINDOW * SOURCES, TILE, TILE), BF16),
            pltpu.VMEM((SLOTS, TILE, TILE), BF16),
            pltpu.VMEM((SOURCES * TILE, 128), F32),
            pltpu.VMEM((WINDOW, 8, 128), F32),
            pltpu.VMEM((SLOTS, TILE), F32),
            pltpu.VMEM((WINDOW, SLOTS), BF16),
            pltpu.VMEM((SOURCES, 16, TILE), BF16),
            pltpu.VMEM((8, 16, TILE), BF16),
            pltpu.VMEM((2, 2 * WINDOW, 128), F32),
            pltpu.VMEM((2, 2 * WINDOW, 128), F32),
            pltpu.VMEM((WINDOW, 1, TILE), F32),
            pltpu.VMEM((1, TILE), F32),
            pltpu.VMEM((1, SLOTS), jnp.int32),
            pltpu.SMEM((1, SLOTS), jnp.int32),
            dma,
            dma((40,)), dma((40,)),
            dma((WINDOW,)), dma((WINDOW,)),
            dma((3,)), dma((3,)),
        ],
        compiler_params=pltpu.CompilerParams(
            collective_id=0, has_side_effects=True, vmem_limit_bytes=62 * 2**20
        ),
    )(source, target, pair_source, pair_target, pair_count)
    return jnp.log(float(TILE) / row_sums.reshape(SOURCES * TILE)), jnp.log(float(SOURCES) / column_sums.reshape(TILE))


def solution(mesh):
    placed = (
        P(("group", "member"), None),
        P(("group", "member"), None),
        P(("group", "member"), None),
        P(("group", "member"), None),
        P(("group", "member")),
    )
    return jax.shard_map(
        shards,
        mesh=mesh,
        in_specs=placed,
        out_specs=(P(("group", "member")), P(("group", "member"))),
        check_vma=False,
    )
```
